32 devices in a mesh: dp: 16 (over z, x, core), tensor: 2 (over y).
Axes of the slice: x: 2, y: 2, z: 4, core: 2. Of those that a mesh axis runs over, the one named last changes fastest.
Arguments:
- q_new: bfloat16 [2048, 8192], P(('dp', 'tensor')), may hold values from -6 to 6
- k_new: bfloat16 [2048, 1024], P(('dp', 'tensor')), may hold values from -8 to 8
- v_new: bfloat16 [2048, 1024], P(('dp', 'tensor')), may hold values from -6 to 6
- hist_kv: bfloat16 [512, 128, 2, 1024], P('dp', None, None, 'tensor'), may hold values from -8 to 8
- sources: int32 [16, 64, 1], P('dp'), may hold values from 0 to 15; in each aligned block of 64 rows (0 to 63, 64 to 127, ..., all dimensions but the last counted through in order) at most 8 rows name the same one
- block_ids: int32 [16, 64], P('dp'), may hold values from 0 to 31
- hist_len: int32 [16], P('dp'), may hold values from 1 to 64, 960 in all
Outputs:
- attended: bfloat16 [2048, 8192], P(('dp', 'tensor'))
The draws below stay inside these ranges and needn't reach their ends.
Inputs may be any that keep to these rules, and one draw needn't show every extreme that they name: `sources`: in each group's list no owner is named in more than 8 slots, and some owner is named in exactly 8 slots. `hist_len`: some group has all 64 slots live.
All inputs are finite; a program needn't handle non-finite values.
Results may differ from the reference program's by a relative error of at most 0.0032.
Values may be sent and summed in bfloat16 or wider, within the bound.
A program may use at most 128 MiB of HBM per device.

```python
import math
import jax
import jax.numpy as jnp
import numpy as np
from jax import lax

HQ = 64
KVH = 8
HD = 128
NEW = 128
HMAX = 64
BLOCK = 128
POOL = 32
CAP = 8
GROUPS = 16
TOKENS = 2048
HIST_BLOCKS = 512
N_DP = 16


def draw_q_new(key, part):
    shape = (TOKENS, HQ * HD)
    values = jnp.clip(jax.random.normal(jax.random.fold_in(key, 1), shape, jnp.float32), -6.0, 6.0)
    return values.astype(jnp.bfloat16)


def draw_hist_kv(key, part):
    shape = (HIST_BLOCKS, BLOCK, KVH * HD)
    keys_part = jnp.clip(2.5 * jax.random.normal(jax.random.fold_in(key, 2), shape, jnp.float32), -8.0, 8.0)
    vals_part = jnp.clip(jax.random.normal(jax.random.fold_in(key, 3), shape, jnp.float32), -6.0, 6.0)
    return jnp.stack([keys_part, vals_part], axis=2).astype(jnp.bfloat16)


def plant(entries, rng, least, high):
    longest = entries.shape.index(max(entries.shape))
    spots = []
    for shift in (0, 1):
        where = [jax.random.randint(jax.random.fold_in(rng, axis), (), 0, length) for axis, length in enumerate(entries.shape)]
        where[longest] = (where[longest] + shift) % entries.shape[longest]
        spots.append(tuple(where))
    return entries.at[spots[0]].set(least).at[spots[1]].set(high)


def shard_levels(key, extent, shards, low, top_value):
    factor_of, own = 1.0, jax.random.fold_in(key, 6)
    for dim, shards_of in shards:
        heights = jnp.exp(jax.random.uniform(jax.random.fold_in(own, dim), (shards_of,), jnp.float32, low / len(shards), top_value / len(shards)))
        factor_of = factor_of * jnp.repeat(heights, extent[dim] // shards_of).reshape([-1 if axis == dim else 1 for axis in range(len(extent))])
    return factor_of


def length_profile(count, total, reach, lean):
    portions = [(1 << 20) // math.isqrt(standing ** lean) + 1 for standing in range(2, count + 1)]
    surplus, holding = total - reach - (count - 1), [1] * (count - 1)
    while surplus > 0:
        movable = [i for i in range(count - 1) if holding[i] < reach]
        pool, budget = sum([portions[i] for i in movable]), surplus
        for i in movable:
            addition = min(reach - holding[i], max(1, budget * portions[i] // pool), surplus)
            holding[i] = holding[i] + addition
            surplus = surplus - addition
    return np.array([reach] + holding)


def ragged_sizes(rng, count, total, reach, lean):
    if count == 2:
        one = jax.random.randint(rng, (), max(1, total - reach), min(reach, total - 1) + 1)
        return jnp.stack([one, total - one])
    lengths = jnp.asarray(length_profile(count, total, reach, lean), jnp.int32)
    couples = (count - 1) // 2
    giver, receiver = lengths[1:1 + 2 * couples:2], lengths[2:2 + 2 * couples:2]
    slack = jnp.minimum(giver - 1, reach - receiver)
    passed = jax.random.randint(jax.random.fold_in(rng, 1), (couples,), 0, 1 << 20) % (slack + 1)
    lengths = lengths.at[1:1 + 2 * couples:2].set(giver - passed).at[2:2 + 2 * couples:2].set(receiver + passed)
    return lengths[jax.random.permutation(jax.random.fold_in(rng, 2), count)]


def assign_block(rng, own, number, rows, amount, top, limit, skew):
    order = jax.random.permutation(rng, amount)
    heavy_load, common = load_shares(amount, rows * top, limit, skew, True), load_shares(amount, rows * top, limit, skew, False)
    places = jnp.arange(amount)

    def named(lengths, turn):
        used = int((lengths > 0).sum())
        fixed = max(1, used // 4)
        shifted = fixed + (places - fixed + turn * (used - fixed)) % max(1, amount - fixed)
        return jnp.zeros((amount,), jnp.int32).at[order[jnp.where(places < fixed, places, shifted)]].set(jnp.asarray(lengths, jnp.int32))

    lengths = jnp.where(number % 4 == 0, named(heavy_load, number // 4), named(common, number - number // 4 - 1))
    mixed = jax.random.permutation(jax.random.fold_in(own, 3), amount)
    source_of, receiver = mixed[0:amount // 2 * 2:2], mixed[1:amount // 2 * 2:2]
    margin = jnp.minimum(lengths[source_of] - 1, limit - lengths[receiver]) // 2
    margin = jnp.where((source_of == order[0]) | (receiver == order[0]) | (lengths[receiver] == 0), 0, jnp.maximum(margin, 0))
    shifted = jax.random.randint(jax.random.fold_in(own, 4), (amount // 2,), 0, 1 << 20) % (margin + 1)
    lengths = lengths.at[source_of].add(-shifted).at[receiver].add(shifted)
    members = jnp.searchsorted(jnp.cumsum(lengths), jnp.arange(rows * top), side="right").astype(jnp.int32)
    table = members.reshape(top, rows).T
    table = table[jax.random.permutation(jax.random.fold_in(own, 1), rows)]
    turn = jax.random.randint(jax.random.fold_in(own, 2), (rows, 1), 0, top)
    return jnp.take_along_axis(table, (jnp.arange(top)[None, :] + turn) % top, axis=1)


def load_shares(count, total, limit, slope, full):
    weights = [(1 << 20) // math.isqrt(grade ** slope) + 1 for grade in range(1, count + 1)]
    largest = limit if full else min(limit, max(-(-total // count), total * weights[0] // sum(weights)))
    least = 1 if total - largest >= count - 1 else 0
    given, spare = [largest] + [least] * (count - 1), total - largest - least * (count - 1)
    while spare > 0:
        movable = [i for i in range(1, count) if given[i] < largest] or [i for i in range(1, count) if given[i] < limit]
        mass, left = sum([weights[i] for i in movable]), spare
        for i in movable:
            addition = min(limit - given[i], max(1, left * weights[i] // mass), spare)
            given[i] = given[i] + addition
            spare = spare - addition
    return np.array(given)


def gaussian(rng, extent, width, bound, shards=(), held_as=jnp.bfloat16):
    array = width * jax.random.normal(rng, extent, jnp.float32)
    if shards:
        array = array * shard_levels(rng, extent, shards, -0.22, 0.18)
    return jnp.clip(array, -bound, bound).astype(held_as)


def setup_inputs(seed: int = 0) -> dict:
    key_of = jax.random.split(jax.random.key(seed), 8)
    q_new = draw_q_new(jax.random.fold_in(key_of[7], 71), 0)
    k_new = gaussian(key_of[1], (TOKENS, KVH * HD), 2.5, 8.0, ((0, 32),))
    v_new = gaussian(key_of[2], (TOKENS, KVH * HD), 1.0, 6.0, ((0, 32),))
    hist_kv = draw_hist_kv(jax.random.fold_in(key_of[7], 71), 0)
    sources_keys = jax.random.split(jax.random.fold_in(key_of[4], 1), GROUPS * HMAX // HMAX)
    sources_turns = jax.random.permutation(jax.random.fold_in(key_of[4], 3), GROUPS * HMAX // HMAX)
    sources = jax.vmap(lambda own, number: assign_block(jax.random.fold_in(key_of[4], 2), own, number, HMAX, N_DP, 1, CAP, 2))(sources_keys, sources_turns).reshape((GROUPS, HMAX, 1))
    block_ids = plant(jax.random.randint(key_of[5], (GROUPS, HMAX), 0, POOL), jax.random.fold_in(key_of[5], 1), 0, POOL - 1).astype(jnp.int32)
    hist_len = ragged_sizes(key_of[6], GROUPS, HMAX * N_DP * 15 // 16, HMAX, 2).astype(jnp.int32)
    return {"q_new": q_new, "k_new": k_new, "v_new": v_new, "hist_kv": hist_kv, "sources": sources, "block_ids": block_ids, "hist_len": hist_len}


def reference(q_new, k_new, v_new, hist_kv, sources, block_ids, hist_len):
    group_count = hist_len.shape[0]
    per_kv = HQ // KVH
    score_scale = 1.0 / math.sqrt(HD)

    def one_group(g):
        query_rows = lax.dynamic_slice_in_dim(q_new, g * NEW, NEW, 0).reshape(NEW, KVH, per_kv, HD).astype(jnp.float32)
        fresh_turn_keys = lax.dynamic_slice_in_dim(k_new, g * NEW, NEW, 0).reshape(NEW, KVH, HD).astype(jnp.float32)
        fresh_turn_values = lax.dynamic_slice_in_dim(v_new, g * NEW, NEW, 0).reshape(NEW, KVH, HD).astype(jnp.float32)
        rows = (sources[g, :, 0] * POOL + block_ids[g]).astype(jnp.int32)
        blocks = hist_kv[rows]
        old_keys = blocks[:, :, 0].reshape(HMAX * BLOCK, KVH, HD).astype(jnp.float32)
        prior_turn_values = blocks[:, :, 1].reshape(HMAX * BLOCK, KVH, HD).astype(jnp.float32)
        live = jnp.repeat(jnp.arange(HMAX) < hist_len[g], BLOCK)
        old_scores = jnp.einsum('nhgd,khd->hgnk', query_rows, old_keys) * score_scale
        old_scores = jnp.where(live[None, None, None, :], old_scores, -jnp.inf)
        causal = jnp.arange(NEW)[:, None] >= jnp.arange(NEW)[None, :]
        fresh_turn_scores = jnp.einsum('fusi,pui->usfp', query_rows, fresh_turn_keys) * score_scale
        fresh_turn_scores = jnp.where(causal[None, None], fresh_turn_scores, -jnp.inf)
        top = jnp.maximum(lax.optimization_barrier(jnp.max(old_scores, axis=-1)), lax.optimization_barrier(jnp.max(fresh_turn_scores, axis=-1)))
        old_weights = jnp.exp(old_scores - top[..., None])
        new_weights = jnp.exp(fresh_turn_scores - top[..., None])
        total = lax.optimization_barrier(jnp.sum(old_weights, axis=-1)) + lax.optimization_barrier(jnp.sum(new_weights, axis=-1))
        prior_pass_result = lax.optimization_barrier(old_weights.astype(jnp.bfloat16)).astype(jnp.float32)
        fresh_pass_result = lax.optimization_barrier(new_weights.astype(jnp.bfloat16)).astype(jnp.float32)
        running_sum = jnp.einsum('cmxf,fcu->cmxu', prior_pass_result, prior_turn_values) + jnp.einsum('qaou,uql->qaol', fresh_pass_result, fresh_turn_values)
        result = running_sum / total[..., None]
        result = jnp.transpose(result, (2, 0, 1, 3)).reshape(NEW, HQ * HD)
        return result.astype(jnp.bfloat16)
    outputs = lax.map(one_group, jnp.arange(group_count, dtype=jnp.int32))
    return outputs.reshape(group_count * NEW, HQ * HD)
```

```python
import functools
import math

import jax
import jax.numpy as jnp
from jax import lax
from jax.experimental import pallas as pl
from jax.experimental.pallas import tpu as pltpu
from jax.sharding import PartitionSpec as P

HD = 128
PER_KV = 8
ROWS = 1024
LOW = -1e30
SCALE = 1.4426950408889634 / math.sqrt(HD)
STEP = 256


def attend_kernel(width, counts, ids, own, q_ref, k_ref, vt_ref, o_ref, st_ref, s_scr, o_acc):
    g = pl.program_id(0)
    n = counts[g]
    total = n + own[g]
    heads = q_ref.shape[1]
    pieces = ROWS // STEP
    st_ref[...] = jnp.zeros_like(st_ref)
    for c in range(heads):

        def score(i, tops, causal):
            keys = k_ref[ids[g * width + i], c]
            out = []
            for j in range(pieces):
                cols = pl.ds(j * STEP, STEP)
                s = jnp.dot(keys, q_ref[0, c, :, cols], preferred_element_type=jnp.float32)
                if causal:
                    row = lax.broadcasted_iota(jnp.int32, s.shape, 0)
                    col = lax.broadcasted_iota(jnp.int32, s.shape, 1)
                    s = jnp.where(row <= col % 128, s, LOW)
                s_scr[i, :, cols] = s
                out.append(jnp.maximum(tops[j], jnp.max(s.reshape(16, 8, STEP), axis=0)))
            return tuple(out)

        tops = tuple(jnp.full((8, STEP), LOW, jnp.float32) for _ in range(pieces))
        tops = lax.fori_loop(0, n, functools.partial(score, causal=False), tops)
        tops = lax.fori_loop(n, total, functools.partial(score, causal=True), tops)

        @pl.when(total % 2 == 1)
        def _():
            s_scr[total] = jnp.zeros_like(s_scr[total])

        shift = [jnp.max(t, axis=0, keepdims=True) * SCALE for t in tops]
        o_acc[...] = jnp.zeros_like(o_acc)

        def gather(pair, sums):
            first = 2 * pair
            second = first + 1
            vt = jnp.concatenate(
                [vt_ref[ids[g * width + first], c], vt_ref[ids[g * width + second], c]], axis=1
            )
            out = []
            for j in range(pieces):
                cols = pl.ds(j * STEP, STEP)
                far = jnp.where(second < total, shift[j], -LOW)
                w0 = jnp.exp2(s_scr[first, :, cols] * SCALE - shift[j])
                w1 = jnp.exp2(s_scr[second, :, cols] * SCALE - far)
                w = jnp.concatenate([w0, w1], axis=0)
                out.append(sums[j] + jnp.sum(w.reshape(32, 8, STEP), axis=0))
                o_acc[:, cols] += jnp.dot(
                    vt, w.astype(jnp.bfloat16), preferred_element_type=jnp.float32
                )
            return tuple(out)

        sums = tuple(jnp.zeros((8, STEP), jnp.float32) for _ in range(pieces))
        sums = lax.fori_loop(0, (total + 1) // 2, gather, sums)
        o_ref[0, c] = o_acc[...].astype(jnp.bfloat16)
        for j in range(pieces):
            cols = pl.ds(j * STEP, STEP)
            st_ref[0, 2 * c : 2 * c + 1, cols] = shift[j]
            st_ref[0, 2 * c + 1 : 2 * c + 2, cols] = jnp.sum(sums[j], axis=0, keepdims=True)


def attend(counts, ids, own, q, keys, vals_t):
    groups, heads = q.shape[:2]
    width = ids.shape[1]
    return pl.pallas_call(
        functools.partial(attend_kernel, width),
        grid_spec=pltpu.PrefetchScalarGridSpec(
            num_scalar_prefetch=3,
            grid=(groups,),
            in_specs=[
                pl.BlockSpec((1, heads, HD, ROWS), lambda g, *_: (g, 0, 0, 0)),
                pl.BlockSpec(memory_space=pltpu.VMEM),
                pl.BlockSpec(memory_space=pltpu.VMEM),
            ],
            out_specs=[
                pl.BlockSpec((1, heads, HD, ROWS), lambda g, *_: (g, 0, 0, 0)),
                pl.BlockSpec((1, 8, ROWS), lambda g, *_: (g, 0, 0)),
            ],
            scratch_shapes=[
                pltpu.VMEM((width, 128, ROWS), jnp.float32),
                pltpu.VMEM((HD, ROWS), jnp.float32),
            ],
        ),
        out_shape=[
            jax.ShapeDtypeStruct(q.shape, jnp.bfloat16),
            jax.ShapeDtypeStruct((groups, 8, ROWS), jnp.float32),
        ],
        compiler_params=pltpu.CompilerParams(vmem_limit_bytes=48 * 1024 * 1024),
    )(counts, ids.reshape(-1), own, q, keys, vals_t)


def exchange(x, axis, groups=None, split=0, concat=0):
    return lax.all_to_all(
        x, axis, split_axis=split, concat_axis=concat, tiled=True, axis_index_groups=groups
    )


def local(q_new, k_new, v_new, hist_kv, sources, block_ids, hist_len):
    groups = lax.axis_size("dp")
    parts = lax.axis_size("tensor")
    tok = q_new.shape[0]
    new = parts * tok
    pool, block = hist_kv.shape[:2]
    slots = block_ids.shape[1]
    kv_heads = hist_kv.shape[3] // HD
    span = 2 if kv_heads % 2 == 0 else 1
    heads = kv_heads // span
    kv_cols = heads * HD
    q_cols = kv_cols * PER_KV
    units = groups // span
    mates = [list(range(span * i, span * i + span)) for i in range(units)]
    peers = [list(range(i, groups, span)) for i in range(span)]
    unit = lax.axis_index("dp") // span

    live = jnp.arange(slots)[None, :] < hist_len[:, None]
    code = jnp.where(live, sources.reshape(1, slots) * pool + block_ids, -1)
    code = lax.all_gather(code, "dp", axis=0, tiled=True)
    mine = (code >= 0) & (code // (span * pool) == unit)
    counts = jnp.sum(mine.astype(jnp.int32), axis=1)
    rank = jnp.cumsum(mine.astype(jnp.int32), axis=1) - 1
    width = min(span * max(2, 2 * slots // groups), slots) + 2
    hit = mine[:, None, :] & (rank[:, None, :] == jnp.arange(width)[None, :, None])
    ids = jnp.sum(jnp.where(hit, (code % (span * pool))[:, None, :], 0), axis=-1)
    order = jnp.arange(groups)
    own = (order // span == unit).astype(jnp.int32)
    extra = (jnp.arange(width)[None, :] == counts[:, None]) & (own[:, None] == 1)
    ids = jnp.where(extra, span * pool + (order % span)[:, None], ids)

    share = parts * span
    turn = jnp.concatenate([x.reshape(tok, share, -1) for x in (q_new, k_new, v_new)], axis=2)
    turn = exchange(turn.reshape(tok, parts, -1), "tensor", split=1)
    turn = turn.reshape(new, span, -1).transpose(1, 0, 2)
    if span > 1:
        turn = exchange(turn, "dp", mates)
    q_t = turn[:, :, :q_cols].reshape(span, new, heads, PER_KV, HD).transpose(0, 2, 4, 3, 1)
    q_t = q_t.reshape(span, heads, HD, PER_KV * new)
    fresh = turn[:, :, q_cols:].reshape(span, new, 2, heads, HD)
    k_fresh = fresh[:, :, 0].transpose(0, 2, 1, 3)
    v_fresh = fresh[:, :, 1].transpose(0, 2, 3, 1)
    q_all = lax.all_gather(q_t, "dp", axis=0, tiled=True, axis_index_groups=peers)

    halves = hist_kv.reshape(pool, block, 2, span, kv_cols).transpose(3, 0, 2, 1, 4)
    if span > 1:
        halves = exchange(halves, "dp", mates)
    halves = halves.reshape(span * pool, 2, block, heads, HD)
    keys = jnp.concatenate([halves[:, 0].transpose(0, 2, 1, 3), k_fresh], axis=0)
    vals_t = jnp.concatenate([halves[:, 1].transpose(0, 2, 3, 1), v_fresh], axis=0)

    part, stats = attend(counts, ids, own, q_all, keys, vals_t)

    part = part.reshape(units, span, heads, HD, ROWS)
    stats = stats[:, : 2 * heads].reshape(units, span, heads, 2, ROWS)
    part = exchange(part, "dp", peers)
    stats = exchange(stats, "dp", peers)
    shift, sums = stats[:, :, :, 0], stats[:, :, :, 1]
    scale = jnp.exp2(shift - jnp.max(shift, axis=0, keepdims=True))
    scale = scale / jnp.sum(scale * sums, axis=0, keepdims=True)
    result = jnp.sum(part.astype(jnp.float32) * scale[:, :, :, None, :], axis=0)
    result = result.astype(jnp.bfloat16)
    result = result.reshape(span, heads, HD, PER_KV, new).transpose(0, 4, 1, 3, 2)
    result = result.reshape(span, new, q_cols)
    if span > 1:
        result = exchange(result, "dp", mates)
    result = result.transpose(1, 0, 2).reshape(new, 1, span * q_cols)
    result = exchange(result, "tensor", split=0, concat=1)
    return result.reshape(tok, share * q_cols)


def solution(mesh):
    return jax.shard_map(
        local,
        mesh=mesh,
        in_specs=(
            P(("dp", "tensor"), None),
            P(("dp", "tensor"), None),
            P(("dp", "tensor"), None),
            P("dp", None, None, "tensor"),
            P("dp", None, None),
            P("dp", None),
            P("dp"),
        ),
        out_specs=P(("dp", "tensor"), None),
        check_vma=False,
    )
```

```python
import functools
import math

import jax
import jax.numpy as jnp
from jax import lax
from jax.experimental import pallas as pl
from jax.experimental.pallas import tpu as pltpu
from jax.sharding import PartitionSpec as P

HD = 128
PER_KV = 8
ROWS = 1024
LOW = -1e30
SCALE = 1.4426950408889634 / math.sqrt(HD)
STEP = 256
EXTRA = 16


def attend_kernel(width, fresh, qsel, gsel, counts, ids, q_ref, k_ref, vt_ref, *rest):
    if fresh:
        kf_ref, vf_ref, *rest = rest
    o_ref, q_t, acc = rest[-3:]
    i = pl.program_id(0)
    g = gsel[i]
    n = counts[g]
    heads = o_ref.shape[1]
    tiles = [(c, j) for c in range(heads) for j in range(ROWS // STEP)]

    for c in range(heads):
        for h in range(PER_KV):
            at = (c * PER_KV + h) * HD
            q_t[c, :, h * 128 : (h + 1) * 128] = q_ref[0, :, at : at + HD].T

    def fold(keys, vals_t, mask, second, carry):
        out = []
        for (c, j), (top, total) in zip(tiles, carry):
            cols = pl.ds(j * STEP, STEP)
            s = jnp.dot(keys[c], q_t[c, :, cols], preferred_element_type=jnp.float32)
            if mask is not None:
                s = jnp.where(mask, s, LOW)
            here = jnp.max(s[:128], axis=0, keepdims=True)
            if second is not None:
                there = jnp.max(s[128:], axis=0, keepdims=True)
                here = jnp.maximum(here, jnp.where(second, there, LOW))
            new = jnp.maximum(top, here * SCALE)
            w = jnp.exp2(s[:128] * SCALE - new)
            if second is not None:
                far = jnp.where(second, new, -LOW)
                w = jnp.concatenate([w, jnp.exp2(s[128:] * SCALE - far)], axis=0)
            fade = jnp.exp2(top - new)
            total = total * fade + jnp.sum(w.reshape(w.shape[0] // 8, 8, STEP), axis=0)
            acc[c, :, cols] = acc[c, :, cols] * fade + jnp.dot(
                vals_t[c], w.astype(jnp.bfloat16), preferred_element_type=jnp.float32
            )
            out.append((new, total))
        return tuple(out)

    acc[...] = jnp.zeros_like(acc)
    carry = tuple(
        (jnp.full((1, STEP), LOW, jnp.float32), jnp.zeros((8, STEP), jnp.float32)) for _ in tiles
    )
    if fresh:
        row = lax.broadcasted_iota(jnp.int32, (128, STEP), 0)
        col = lax.broadcasted_iota(jnp.int32, (128, STEP), 1)
        carry = fold(
            [kf_ref[i, c] for c in range(heads)],
            [vf_ref[i, c] for c in range(heads)],
            row <= col % 128,
            None,
            carry,
        )

    def pair(p, carry):
        one, two = ids[g * width + 2 * p], ids[g * width + 2 * p + 1]
        return fold(
            [jnp.concatenate([k_ref[one, c], k_ref[two, c]], axis=0) for c in range(heads)],
            [jnp.concatenate([vt_ref[one, c], vt_ref[two, c]], axis=1) for c in range(heads)],
            None,
            2 * p + 1 < n,
            carry,
        )

    carry = lax.fori_loop(0, (n + 1) // 2, pair, carry)
    for (c, j), (top, total) in zip(tiles, carry):
        cols = pl.ds(j * STEP, STEP)
        total = jnp.sum(total, axis=0, keepdims=True)
        some = total > 0.0
        safe = jnp.where(some, total, 1.0)
        o_ref[0, c, :HD, cols] = (acc[c, :, cols] / safe).astype(o_ref.dtype)
        left = jnp.where(some, top + jnp.log2(safe), LOW)
        row = lax.broadcasted_iota(jnp.int32, (EXTRA, STEP), 0)
        terms = jnp.zeros((EXTRA, STEP), jnp.float32)
        for k in range(3):
            term = left.astype(jnp.bfloat16).astype(jnp.float32)
            terms = jnp.where(row == k, term, terms)
            left = left - term
        o_ref[0, c, HD:, cols] = terms.astype(o_ref.dtype)


def attend(qsel, gsel, counts, ids, q, keys, vals_t, fresh=None, after=None):
    count = qsel.shape[0]
    heads = keys.shape[1]
    width = ids.shape[1]
    extra = () if fresh is None else fresh
    behind = () if after is None else (after,)
    work = count * 8 * heads * ROWS * 128
    return pl.pallas_call(
        functools.partial(attend_kernel, width, fresh is not None),
        grid_spec=pltpu.PrefetchScalarGridSpec(
            num_scalar_prefetch=4,
            grid=(count,),
            in_specs=[pl.BlockSpec((1,) + q.shape[1:], lambda i, qs, *_: (qs[i], 0, 0))]
            + [pl.BlockSpec(memory_space=pltpu.VMEM)] * (2 + len(extra))
            + [pl.BlockSpec(memory_space=pl.ANY)] * len(behind),
            out_specs=pl.BlockSpec((1, heads, HD + EXTRA, ROWS), lambda i, *_: (i, 0, 0, 0)),
            scratch_shapes=[
                pltpu.VMEM((heads, HD, ROWS), jnp.bfloat16),
                pltpu.VMEM((heads, HD, ROWS), jnp.float32),
            ],
        ),
        out_shape=jax.ShapeDtypeStruct(
            (count, heads, HD + EXTRA, ROWS), jnp.bfloat16 if fresh is None else jnp.float32
        ),
        compiler_params=pltpu.CompilerParams(vmem_limit_bytes=28 * 1024 * 1024),
        cost_estimate=pl.CostEstimate(
            flops=4 * HD * work, bytes_accessed=4 * count * heads * HD * ROWS, transcendentals=work
        ),
    )(qsel, gsel, counts, ids.reshape(-1), q, keys, vals_t, *extra, *behind)


def exchange(x, axis, groups=None, split=0, concat=0):
    return lax.all_to_all(
        x, axis, split_axis=split, concat_axis=concat, tiled=True, axis_index_groups=groups
    )


def local(q_new, k_new, v_new, hist_kv, sources, block_ids, hist_len):
    groups = lax.axis_size("dp")
    parts = lax.axis_size("tensor")
    tok = q_new.shape[0]
    new = parts * tok
    pool, block = hist_kv.shape[:2]
    slots = block_ids.shape[1]
    kv_heads = hist_kv.shape[3] // HD
    span = 2 if kv_heads % 2 == 0 else 1
    heads = kv_heads // span
    kv_cols = heads * HD
    q_cols = kv_cols * PER_KV
    units = groups // span
    mates = [list(range(span * i, span * i + span)) for i in range(units)]
    peers = [list(range(i, groups, span)) for i in range(span)]
    unit = lax.axis_index("dp") // span

    live = jnp.arange(slots)[None, :] < hist_len[:, None]
    code = jnp.where(live, sources.reshape(1, slots) * pool + block_ids, -1)
    code = lax.all_gather(code, "dp", axis=0, tiled=True)
    mine = (code >= 0) & (code // (span * pool) == unit)
    counts = jnp.sum(mine.astype(jnp.int32), axis=1)
    rank = jnp.cumsum(mine.astype(jnp.int32), axis=1) - 1
    width = min(span * max(2, 2 * slots // groups), slots) + 2
    hit = mine[:, None, :] & (rank[:, None, :] == jnp.arange(width)[None, :, None])
    ids = jnp.sum(jnp.where(hit, (code % (span * pool))[:, None, :], 0), axis=-1)

    share = parts * span
    turn = jnp.concatenate([x.reshape(tok, share, -1) for x in (q_new, k_new, v_new)], axis=2)
    turn = exchange(turn.reshape(tok, parts, -1), "tensor", split=1)
    turn = turn.reshape(new, span, -1).transpose(1, 0, 2)
    if span > 1:
        turn = exchange(turn, "dp", mates)
    q = turn[:, :, :q_cols]
    q_all = lax.all_gather(q, "dp", axis=0, tiled=True, axis_index_groups=peers)
    fresh = turn[:, :, q_cols:].reshape(span, new, 2, heads, HD)
    k_fresh = fresh[:, :, 0].transpose(0, 2, 1, 3)
    v_fresh = fresh[:, :, 1].transpose(0, 2, 3, 1)

    halves = hist_kv.reshape(pool, block, 2, span, kv_cols).transpose(3, 0, 2, 1, 4)
    if span > 1:
        halves = exchange(halves, "dp", mates)
    halves = halves.reshape(span * pool, 2, block, heads, HD)
    keys = halves[:, 0].transpose(0, 2, 1, 3)
    vals_t = halves[:, 1].transpose(0, 2, 3, 1)

    core = jnp.arange(span, dtype=jnp.int32)
    own = attend(core, unit * span + core, counts, ids, q, keys, vals_t, (k_fresh, v_fresh))
    arrived, sent = [own], []
    apart = list(range(units - 1, 0, -1))
    per = max(1, units // 8)
    for at in range(0, len(apart), per):
        some = apart[at : at + per]
        sel = jnp.concatenate([(unit ^ r) * span + core for r in some])
        after = own if len(sent) < 4 else sent[-4]
        part = attend(sel, sel, counts, ids, q_all, keys, vals_t, after=after)
        for k, r in enumerate(some):
            to = [(u * span + c, (u ^ r) * span + c) for u in range(units) for c in range(span)]
            arrived.append(lax.ppermute(part[k * span : (k + 1) * span], "dp", to))
        sent.append(arrived[-1])
    arrived = [x.astype(jnp.float32) for x in arrived]
    lses = [x[:, :, HD] + x[:, :, HD + 1] + x[:, :, HD + 2] for x in arrived]
    top = functools.reduce(jnp.maximum, lses)
    scales = [jnp.exp2(lse - top) for lse in lses]
    total = sum(scales)
    result = sum(x[:, :, :HD] * (w / total)[:, :, None, :] for x, w in zip(arrived, scales))
    result = result.astype(jnp.bfloat16)
    result = result.reshape(span, heads, HD, PER_KV, new).transpose(0, 4, 1, 3, 2)
    result = result.reshape(span, new, q_cols)
    if span > 1:
        result = exchange(result, "dp", mates)
    result = result.transpose(1, 0, 2).reshape(new, 1, span * q_cols)
    result = exchange(result, "tensor", split=0, concat=1)
    return result.reshape(tok, share * q_cols)


def solution(mesh):
    return jax.shard_map(
        local,
        mesh=mesh,
        in_specs=(
            P(("dp", "tensor"), None),
            P(("dp", "tensor"), None),
            P(("dp", "tensor"), None),
            P("dp", None, None, "tensor"),
            P("dp", None, None),
            P("dp", None),
            P("dp"),
        ),
        out_specs=P(("dp", "tensor"), None),
        check_vma=False,
    )
```

```python
import functools
import math

import jax
import jax.numpy as jnp
from jax import lax
from jax.experimental import pallas as pl
from jax.experimental.pallas import tpu as pltpu
from jax.sharding import PartitionSpec as P

HD = 128
PER_KV = 8
ROWS = 1024
LOW = -1e30
SCALE = 1.4426950408889634 / math.sqrt(HD)
STEP = 256
EXTRA = 16


def attend_kernel(width, fresh, qsel, gsel, counts, ids, q_ref, k_ref, vt_ref, *rest):
    if fresh:
        kf_ref, vf_ref, *rest = rest
    o_ref, acc = rest[-2:]
    i = pl.program_id(0)
    g = gsel[i]
    n = counts[g]
    heads = o_ref.shape[1]
    tiles = [(c, j) for c in range(heads) for j in range(ROWS // STEP)]

    def fold(keys, vals_t, mask, second, carry):
        out = []
        for (c, j), (top, total) in zip(tiles, carry):
            cols = pl.ds(j * STEP, STEP)
            s = jnp.dot(keys[c], q_ref[0, c, :, cols], preferred_element_type=jnp.float32)
            if mask is not None:
                s = jnp.where(mask, s, LOW)
            here = jnp.max(s[:128], axis=0, keepdims=True)
            if second is not None:
                there = jnp.max(s[128:], axis=0, keepdims=True)
                here = jnp.maximum(here, jnp.where(second, there, LOW))
            new = jnp.maximum(top, here * SCALE)
            w = jnp.exp2(s[:128] * SCALE - new)
            if second is not None:
                far = jnp.where(second, new, -LOW)
                w = jnp.concatenate([w, jnp.exp2(s[128:] * SCALE - far)], axis=0)
            fade = jnp.exp2(top - new)
            total = total * fade + jnp.sum(w.reshape(w.shape[0] // 8, 8, STEP), axis=0)
            acc[c, :, cols] = acc[c, :, cols] * fade + jnp.dot(
                vals_t[c], w.astype(jnp.bfloat16), preferred_element_type=jnp.float32
            )
            out.append((new, total))
        return tuple(out)

    acc[...] = jnp.zeros_like(acc)
    carry = tuple(
        (jnp.full((1, STEP), LOW, jnp.float32), jnp.zeros((8, STEP), jnp.float32)) for _ in tiles
    )
    if fresh:
        row = lax.broadcasted_iota(jnp.int32, (128, STEP), 0)
        col = lax.broadcasted_iota(jnp.int32, (128, STEP), 1)
        carry = fold(
            [kf_ref[i, c] for c in range(heads)],
            [vf_ref[i, c] for c in range(heads)],
            row <= col % 128,
            None,
            carry,
        )

    def pair(p, carry):
        one, two = ids[g * width + 2 * p], ids[g * width + 2 * p + 1]
        return fold(
            [jnp.concatenate([k_ref[one, c], k_ref[two, c]], axis=0) for c in range(heads)],
            [jnp.concatenate([vt_ref[one, c], vt_ref[two, c]], axis=1) for c in range(heads)],
            None,
            2 * p + 1 < n,
            carry,
        )

    carry = lax.fori_loop(0, (n + 1) // 2, pair, carry)
    for (c, j), (top, total) in zip(tiles, carry):
        cols = pl.ds(j * STEP, STEP)
        total = jnp.sum(total, axis=0, keepdims=True)
        some = total > 0.0
        safe = jnp.where(some, total, 1.0)
        part = 1.0 / safe
        o_ref[0, c, :HD, cols] = (acc[c, :, cols] * part).astype(o_ref.dtype)
        left = jnp.where(some, top + jnp.log2(safe), LOW)
        row = lax.broadcasted_iota(jnp.int32, (EXTRA, STEP), 0)
        terms = jnp.zeros((EXTRA, STEP), jnp.float32)
        for k in range(3):
            term = left.astype(jnp.bfloat16).astype(jnp.float32)
            terms = jnp.where(row == k, term, terms)
            left = left - term
        o_ref[0, c, HD:, cols] = terms.astype(o_ref.dtype)


def attend(qsel, gsel, counts, ids, q, keys, vals_t, fresh=None, after=None):
    count = qsel.shape[0]
    heads = keys.shape[1]
    width = ids.shape[1]
    extra = () if fresh is None else fresh
    behind = () if after is None else (after,)
    work = count * 8 * heads * ROWS * 128
    return pl.pallas_call(
        functools.partial(attend_kernel, width, fresh is not None),
        grid_spec=pltpu.PrefetchScalarGridSpec(
            num_scalar_prefetch=4,
            grid=(count,),
            in_specs=[pl.BlockSpec((1,) + q.shape[1:], lambda i, qs, *_: (qs[i], 0, 0, 0))]
            + [pl.BlockSpec(memory_space=pltpu.VMEM)] * (2 + len(extra))
            + [pl.BlockSpec(memory_space=pl.ANY)] * len(behind),
            out_specs=pl.BlockSpec((1, heads, HD + EXTRA, ROWS), lambda i, *_: (i, 0, 0, 0)),
            scratch_shapes=[
                pltpu.VMEM((heads, HD, ROWS), jnp.float32),
            ],
        ),
        out_shape=jax.ShapeDtypeStruct(
            (count, heads, HD + EXTRA, ROWS), jnp.bfloat16 if fresh is None else jnp.float32
        ),
        compiler_params=pltpu.CompilerParams(vmem_limit_bytes=28 * 1024 * 1024),
        cost_estimate=pl.CostEstimate(
            flops=4 * HD * work, bytes_accessed=4 * count * heads * HD * ROWS, transcendentals=work
        ),
    )(qsel, gsel, counts, ids.reshape(-1), q, keys, vals_t, *extra, *behind)


def exchange(x, axis, groups=None, split=0, concat=0):
    return lax.all_to_all(
        x, axis, split_axis=split, concat_axis=concat, tiled=True, axis_index_groups=groups
    )


def local(q_new, k_new, v_new, hist_kv, sources, block_ids, hist_len):
    groups = lax.axis_size("dp")
    parts = lax.axis_size("tensor")
    tok = q_new.shape[0]
    new = parts * tok
    pool, block = hist_kv.shape[:2]
    slots = block_ids.shape[1]
    kv_heads = hist_kv.shape[3] // HD
    span = 2 if kv_heads % 2 == 0 else 1
    heads = kv_heads // span
    kv_cols = heads * HD
    q_cols = kv_cols * PER_KV
    units = groups // span
    mates = [list(range(span * i, span * i + span)) for i in range(units)]
    peers = [list(range(i, groups, span)) for i in range(span)]
    unit = lax.axis_index("dp") // span

    live = jnp.arange(slots)[None, :] < hist_len[:, None]
    code = jnp.where(live, sources.reshape(1, slots) * pool + block_ids, -1)
    code = lax.all_gather(code, "dp", axis=0, tiled=True)
    mine = (code >= 0) & (code // (span * pool) == unit)
    counts = jnp.sum(mine.astype(jnp.int32), axis=1)
    rank = jnp.cumsum(mine.astype(jnp.int32), axis=1) - 1
    width = min(span * max(2, 2 * slots // groups), slots) + 2
    hit = mine[:, None, :] & (rank[:, None, :] == jnp.arange(width)[None, :, None])
    ids = jnp.sum(jnp.where(hit, (code % (span * pool))[:, None, :], 0), axis=-1)

    share = parts * span
    turn = jnp.concatenate([x.reshape(tok, share, -1) for x in (q_new, k_new, v_new)], axis=2)
    turn = exchange(turn.reshape(tok, parts, -1), "tensor", split=1)
    turn = turn.reshape(new, span, -1).transpose(1, 0, 2)
    if span > 1:
        turn = exchange(turn, "dp", mates)
    q = turn[:, :, :q_cols].reshape(span, new, heads, PER_KV, HD).transpose(2, 0, 4, 3, 1)
    q = q.reshape(heads, span, 1, HD, PER_KV * new)
    q_all = [
        lax.all_gather(q[c], "dp", axis=0, tiled=True, axis_index_groups=peers)
        for c in range(heads)
    ]
    fresh = turn[:, :, q_cols:].reshape(span, new, 2, heads, 1, HD)
    k_fresh = fresh[:, :, 0].transpose(2, 0, 3, 1, 4)
    v_fresh = fresh[:, :, 1].transpose(2, 0, 3, 4, 1)

    halves = hist_kv.reshape(pool, block, 2, span, kv_cols).transpose(3, 0, 2, 1, 4)
    if span > 1:
        halves = exchange(halves, "dp", mates)
    halves = halves.reshape(span * pool, 2, block, heads, 1, HD)
    keys = halves[:, 0].transpose(2, 0, 3, 1, 4)
    vals_t = halves[:, 1].transpose(2, 0, 3, 4, 1)

    core = jnp.arange(span, dtype=jnp.int32)
    apart = list(range(units - 1, 0, -1))
    per = max(1, units // 8)
    results, sent = [], []
    arrived = [
        [
            attend(
                core, unit * span + core, counts, ids, q[c], keys[c], vals_t[c],
                (k_fresh[c], v_fresh[c]),
            )
        ]
        for c in range(heads)
    ]
    for c in range(heads):
        for at in range(0, len(apart), per):
            some = apart[at : at + per]
            sel = jnp.concatenate([(unit ^ r) * span + core for r in some])
            after = arrived[c][0] if len(sent) < 4 else sent[-4]
            part = attend(sel, sel, counts, ids, q_all[c], keys[c], vals_t[c], after=after)
            for k, r in enumerate(some):
                to = [(u * span + i, (u ^ r) * span + i) for u in range(units) for i in range(span)]
                arrived[c].append(lax.ppermute(part[k * span : (k + 1) * span], "dp", to))
            sent.append(arrived[c][-1])
    for c in range(heads):
        got = [x[:, 0] for x in arrived[c]]
        lses = [jnp.sum(x[:, HD : HD + 3].astype(jnp.float32), axis=1) for x in got]
        top = functools.reduce(jnp.maximum, lses)
        scales = [jnp.exp2(lse - top) for lse in lses]
        total = sum(scales)
        results.append(
            sum(
                x[:, :HD].astype(jnp.float32) * (w / total)[:, None, :]
                for x, w in zip(got, scales)
            )
        )
    result = jnp.stack(results, axis=1)
    result = result.astype(jnp.bfloat16)
    result = result.reshape(span, heads, HD, PER_KV, new).transpose(0, 4, 1, 3, 2)
    result = result.reshape(span, new, q_cols)
    if span > 1:
        result = exchange(result, "dp", mates)
    result = result.transpose(1, 0, 2).reshape(new, 1, span * q_cols)
    result = exchange(result, "tensor", split=0, concat=1)
    return result.reshape(tok, share * q_cols)


def solution(mesh):
    return jax.shard_map(
        local,
        mesh=mesh,
        in_specs=(
            P(("dp", "tensor"), None),
            P(("dp", "tensor"), None),
            P(("dp", "tensor"), None),
            P("dp", None, None, "tensor"),
            P("dp", None, None),
            P("dp", None),
            P("dp"),
        ),
        out_specs=P(("dp", "tensor"), None),
        check_vma=False,
    )
```

```python
import functools
import math

import jax
import jax.numpy as jnp
from jax import lax
from jax.experimental import pallas as pl
from jax.experimental.pallas import tpu as pltpu
from jax.sharding import PartitionSpec as P

HD = 128
PER_KV = 8
ROWS = 1024
LOW = -1e30
SCALE = 1.4426950408889634 / math.sqrt(HD)
STEP = 256
EXTRA = 16
BATCH = 4


def attend_kernel(width, fresh, qsel, gsel, counts, ids, q_ref, k_ref, vt_ref, *rest):
    if fresh:
        kf_ref, vf_ref, *rest = rest
    o_ref, acc, s_scr, w_scr = rest[-4:]
    i = pl.program_id(0)
    g = gsel[i]
    n = counts[g]
    heads = o_ref.shape[1]
    tiles = [(c, j) for c in range(heads) for j in range(ROWS // STEP)]

    def fold(keys, vals_t, mask, alive, carry):
        rows = len(alive) * 128
        news, totals = [], []
        for (c, j), (top, _) in zip(tiles, carry):
            cols = pl.ds(j * STEP, STEP)
            for at in range(0, rows, 256):
                end = min(rows, at + 256)
                s = jnp.dot(
                    keys[c][at:end], q_ref[0, c, :, cols], preferred_element_type=jnp.float32
                )
                s = s * SCALE
                if mask is not None:
                    s = jnp.where(mask, s, LOW)
                s_scr[c, at:end, cols] = s
                for k in range(at, end, 128):
                    here = jnp.max(s[k - at : k - at + 128], axis=0, keepdims=True)
                    if alive[k // 128] is not None:
                        here = jnp.where(alive[k // 128], here, LOW)
                    top = jnp.maximum(top, here)
            news.append(top)
        for (c, j), new, (top, total) in zip(tiles, news, carry):
            cols = pl.ds(j * STEP, STEP)
            total = total * jnp.exp2(top - new)
            for k, live in enumerate(alive):
                at = pl.ds(k * 128, 128)
                far = new if live is None else jnp.where(live, new, -LOW)
                w = jnp.exp2(s_scr[c, at, cols] - far)
                total = total + jnp.sum(w.reshape(16, 8, STEP), axis=0)
                w_scr[c, at, cols] = w.astype(jnp.bfloat16)
            totals.append(total)
        for (c, j), new, (top, _) in zip(tiles, news, carry):
            cols = pl.ds(j * STEP, STEP)
            acc[c, :, cols] = acc[c, :, cols] * jnp.exp2(top - new) + jnp.dot(
                vals_t[c], w_scr[c, :rows, cols], preferred_element_type=jnp.float32
            )
        return tuple(zip(news, totals))

    acc[...] = jnp.zeros_like(acc)
    carry = tuple(
        (jnp.full((1, STEP), LOW, jnp.float32), jnp.zeros((8, STEP), jnp.float32)) for _ in tiles
    )
    if fresh:
        row = lax.broadcasted_iota(jnp.int32, (128, STEP), 0)
        col = lax.broadcasted_iota(jnp.int32, (128, STEP), 1)
        carry = fold(
            [kf_ref[i, c] for c in range(heads)],
            [vf_ref[i, c] for c in range(heads)],
            row <= col % 128,
            [None],
            carry,
        )

    def batch(p, carry):
        which = [ids[g * width + BATCH * p + k] for k in range(BATCH)]
        return fold(
            [jnp.concatenate([k_ref[i, c] for i in which], axis=0) for c in range(heads)],
            [jnp.concatenate([vt_ref[i, c] for i in which], axis=1) for c in range(heads)],
            None,
            [None] + [BATCH * p + k < n for k in range(1, BATCH)],
            carry,
        )

    carry = lax.fori_loop(0, (n + BATCH - 1) // BATCH, batch, carry)
    for (c, j), (top, total) in zip(tiles, carry):
        cols = pl.ds(j * STEP, STEP)
        total = jnp.sum(total, axis=0, keepdims=True)
        some = total > 0.0
        safe = jnp.where(some, total, 1.0)
        part = 1.0 / safe
        o_ref[0, c, :HD, cols] = (acc[c, :, cols] * part).astype(o_ref.dtype)
        left = jnp.where(some, top + jnp.log2(safe), LOW)
        row = lax.broadcasted_iota(jnp.int32, (EXTRA, STEP), 0)
        terms = jnp.zeros((EXTRA, STEP), jnp.float32)
        for k in range(3):
            term = left.astype(jnp.bfloat16).astype(jnp.float32)
            terms = jnp.where(row == k, term, terms)
            left = left - term
        o_ref[0, c, HD:, cols] = terms.astype(o_ref.dtype)


def attend(qsel, gsel, counts, ids, q, keys, vals_t, fresh=None, after=None):
    count = qsel.shape[0]
    heads = keys.shape[1]
    width = ids.shape[1]
    extra = () if fresh is None else fresh
    behind = () if after is None else (after,)
    work = count * 8 * heads * ROWS * 128
    return pl.pallas_call(
        functools.partial(attend_kernel, width, fresh is not None),
        grid_spec=pltpu.PrefetchScalarGridSpec(
            num_scalar_prefetch=4,
            grid=(count,),
            in_specs=[pl.BlockSpec((1,) + q.shape[1:], lambda i, qs, *_: (qs[i], 0, 0, 0))]
            + [pl.BlockSpec(memory_space=pltpu.VMEM)] * (2 + len(extra))
            + [pl.BlockSpec(memory_space=pl.ANY)] * len(behind),
            out_specs=pl.BlockSpec((1, heads, HD + EXTRA, ROWS), lambda i, *_: (i, 0, 0, 0)),
            scratch_shapes=[
                pltpu.VMEM((heads, HD, ROWS), jnp.float32),
                pltpu.VMEM((heads, BATCH * 128, ROWS), jnp.float32),
                pltpu.VMEM((heads, BATCH * 128, ROWS), jnp.bfloat16),
            ],
        ),
        out_shape=jax.ShapeDtypeStruct(
            (count, heads, HD + EXTRA, ROWS), jnp.bfloat16 if fresh is None else jnp.float32
        ),
        compiler_params=pltpu.CompilerParams(vmem_limit_bytes=28 * 1024 * 1024),
        cost_estimate=pl.CostEstimate(
            flops=4 * HD * work, bytes_accessed=4 * count * heads * HD * ROWS, transcendentals=work
        ),
    )(qsel, gsel, counts, ids.reshape(-1), q, keys, vals_t, *extra, *behind)


def exchange(x, axis, groups=None, split=0, concat=0):
    return lax.all_to_all(
        x, axis, split_axis=split, concat_axis=concat, tiled=True, axis_index_groups=groups
    )


def local(q_new, k_new, v_new, hist_kv, sources, block_ids, hist_len):
    groups = lax.axis_size("dp")
    parts = lax.axis_size("tensor")
    tok = q_new.shape[0]
    new = parts * tok
    pool, block = hist_kv.shape[:2]
    slots = block_ids.shape[1]
    kv_heads = hist_kv.shape[3] // HD
    span = 2 if kv_heads % 2 == 0 else 1
    heads = kv_heads // span
    kv_cols = heads * HD
    q_cols = kv_cols * PER_KV
    units = groups // span
    mates = [list(range(span * i, span * i + span)) for i in range(units)]
    peers = [list(range(i, groups, span)) for i in range(span)]
    unit = lax.axis_index("dp") // span

    live = jnp.arange(slots)[None, :] < hist_len[:, None]
    code = jnp.where(live, sources.reshape(1, slots) * pool + block_ids, -1)
    code = lax.all_gather(code, "dp", axis=0, tiled=True)
    mine = (code >= 0) & (code // (span * pool) == unit)
    counts = jnp.sum(mine.astype(jnp.int32), axis=1)
    rank = jnp.cumsum(mine.astype(jnp.int32), axis=1) - 1
    width = min(span * max(2, 2 * slots // groups), slots)
    width = -(-width // BATCH) * BATCH
    hit = mine[:, None, :] & (rank[:, None, :] == jnp.arange(width)[None, :, None])
    ids = jnp.sum(jnp.where(hit, (code % (span * pool))[:, None, :], 0), axis=-1)

    share = parts * span
    turn = jnp.concatenate([x.reshape(tok, share, -1) for x in (q_new, k_new, v_new)], axis=2)
    turn = exchange(turn.reshape(tok, parts, -1), "tensor", split=1)
    turn = turn.reshape(new, span, -1).transpose(1, 0, 2)
    if span > 1:
        turn = exchange(turn, "dp", mates)
    q = turn[:, :, :q_cols].reshape(span, new, heads, PER_KV, HD).transpose(2, 0, 4, 3, 1)
    q = q.reshape(heads, span, 1, HD, PER_KV * new)
    q_all = [
        lax.all_gather(q[c], "dp", axis=0, tiled=True, axis_index_groups=peers)
        for c in range(heads)
    ]
    fresh = turn[:, :, q_cols:].reshape(span, new, 2, heads, 1, HD)
    k_fresh = fresh[:, :, 0].transpose(2, 0, 3, 1, 4)
    v_fresh = fresh[:, :, 1].transpose(2, 0, 3, 4, 1)

    halves = hist_kv.reshape(pool, block, 2, span, kv_cols).transpose(3, 0, 2, 1, 4)
    if span > 1:
        halves = exchange(halves, "dp", mates)
    halves = halves.reshape(span * pool, 2, block, heads, 1, HD)
    keys = halves[:, 0].transpose(2, 0, 3, 1, 4)
    vals_t = halves[:, 1].transpose(2, 0, 3, 4, 1)

    core = jnp.arange(span, dtype=jnp.int32)
    apart = list(range(units - 1, 0, -1))
    per = max(1, units // 8)
    results, sent = [], []
    arrived = [
        [
            attend(
                core, unit * span + core, counts, ids, q[c], keys[c], vals_t[c],
                (k_fresh[c], v_fresh[c]),
            )
        ]
        for c in range(heads)
    ]
    for c in range(heads):
        for at in range(0, len(apart), per):
            some = apart[at : at + per]
            sel = jnp.concatenate([(unit ^ r) * span + core for r in some])
            after = arrived[c][0] if len(sent) < 4 else sent[-4]
            part = attend(sel, sel, counts, ids, q_all[c], keys[c], vals_t[c], after=after)
            for k, r in enumerate(some):
                to = [(u * span + i, (u ^ r) * span + i) for u in range(units) for i in range(span)]
                arrived[c].append(lax.ppermute(part[k * span : (k + 1) * span], "dp", to))
            sent.append(arrived[c][-1])
    for c in range(heads):
        got = [x[:, 0] for x in arrived[c]]
        lses = [jnp.sum(x[:, HD : HD + 3].astype(jnp.float32), axis=1) for x in got]
        top = functools.reduce(jnp.maximum, lses)
        scales = [jnp.exp2(lse - top) for lse in lses]
        total = sum(scales)
        results.append(
            sum(
                x[:, :HD].astype(jnp.float32) * (w / total)[:, None, :]
                for x, w in zip(got, scales)
            )
        )
    result = jnp.stack(results, axis=1)
    result = result.astype(jnp.bfloat16)
    result = result.reshape(span, heads, HD, PER_KV, new).transpose(0, 4, 1, 3, 2)
    result = result.reshape(span, new, q_cols)
    if span > 1:
        result = exchange(result, "dp", mates)
    result = result.transpose(1, 0, 2).reshape(new, 1, span * q_cols)
    result = exchange(result, "tensor", split=0, concat=1)
    return result.reshape(tok, share * q_cols)


def solution(mesh):
    return jax.shard_map(
        local,
        mesh=mesh,
        in_specs=(
            P(("dp", "tensor"), None),
            P(("dp", "tensor"), None),
            P(("dp", "tensor"), None),
            P("dp", None, None, "tensor"),
            P("dp", None, None),
            P("dp", None),
            P("dp"),
        ),
        out_specs=P(("dp", "tensor"), None),
        check_vma=False,
    )
```
